512 devices in a mesh: row: 4 (over x), col: 16 (over z), depth: 8 (over y, core).
Axes of the slice: x: 4, y: 4, z: 16, core: 2. Of those that a mesh axis runs over, the one named last changes fastest.
Arguments:
- inputs: bfloat16 [4096, 2560], P('depth', ('row', 'col')), may hold values from -6 to 6
- w_in: bfloat16 [2560, 10240], P('row', 'col'), may hold values from -0.15625 to 0.15625
- w_out: bfloat16 [10240, 2560], P('col', 'row'), may hold values from -0.078125 to 0.078125
- y_cot: bfloat16 [4096, 2560], P('depth', ('row', 'col')), may hold values from -0.75 to 0.75
Outputs:
- y_out: bfloat16 [4096, 2560], P('depth', ('row', 'col'))
- x_grad: bfloat16 [4096, 2560], P('depth', ('row', 'col'))
- w_in_grad: bfloat16 [2560, 10240], P('row', 'col')
- w_out_grad: bfloat16 [10240, 2560], P('col', 'row')
The draws below stay inside these ranges and needn't reach their ends.
All inputs are finite; a program needn't handle non-finite values.
Results may differ from the reference program's by a relative error of at most 0.029.
Values may be sent and summed in bfloat16 or wider, within the bound.
No kernel may reach another device: no remote copies, remote signals or barrier semaphores. Data moves between devices by JAX's collectives and lax.ppermute only.
A program may use at most 64 MiB of HBM per device.

```python
import jax
import jax.numpy as jnp
from jax import lax

D = 2560
FF = 10240
TOK_DEV = 128
TOKENS = 4096
N_ROW = 4
N_COL = 16
N_DEPTH = 8


def with_spikes(drawn, key, source, target, shards_of, factor):
    owner, partner = [(jnp.arange(drawn.shape[position]) // (drawn.shape[position] // shards_of)).reshape([-1 if axis == position else 1 for axis in range(drawn.ndim)]) for position in (source, target)]
    chosen = jax.random.permutation(key, shards_of)[partner]
    strong = (owner == chosen) | (owner == (partner + shards_of // 2) % shards_of)
    return jnp.where(strong, factor * drawn, drawn)


def shard_levels(stream_key, extent, cuts, low, largest):
    gain, own = 1.0, jax.random.fold_in(stream_key, 6)
    for dim, blocks in cuts:
        steps = jnp.exp(jax.random.uniform(jax.random.fold_in(own, dim), (blocks,), jnp.float32, low / len(cuts), largest / len(cuts)))
        gain = gain * jnp.repeat(steps, extent[dim] // blocks).reshape([-1 if axis == dim else 1 for axis in range(len(extent))])
    return gain


def centred(own_key, extent, width, limit, cuts=(), kind=jnp.bfloat16):
    drawn = width * jax.random.normal(own_key, extent, jnp.float32)
    if cuts:
        drawn = drawn * shard_levels(own_key, extent, cuts, -0.22, 0.18)
    return jnp.clip(drawn, -limit, limit).astype(kind)


def heavy_noise(stream_key, extent, spread, bound, shards, heavy, kind=jnp.bfloat16):
    array = spread * jax.random.normal(stream_key, extent, jnp.float32)
    if shards:
        array = array * shard_levels(stream_key, extent, shards, -0.22, 0.18)
    return jnp.clip(with_spikes(array, jax.random.fold_in(stream_key, 3), *heavy), -bound, bound).astype(kind)


def setup_inputs(seed: int = 0) -> dict:
    streams_of = jax.random.split(jax.random.key(seed), 5)
    inputs = centred(streams_of[0], (TOKENS, D), 1.0, 6.0, ((0, 8), (1, 64)))
    w_in = heavy_noise(streams_of[1], (D, FF), D ** -0.5, 0.15625, ((0, 4), (1, 16)), (1, 0, 16, 2.0))
    w_out = heavy_noise(streams_of[2], (FF, D), FF ** -0.5, 0.078125, ((0, 16), (1, 4)), (0, 1, 16, 2.0))
    y_cot = centred(streams_of[3], (TOKENS, D), (TOKENS ** -0.25), 0.75, ((0, 8), (1, 64)))
    return {"inputs": inputs, "w_in": w_in, "w_out": w_out, "y_cot": y_cot}


gelu_c = 0.7978845608
gelu_a = 0.044715


def gelu_value(h):
    t = jnp.tanh(gelu_c * (h + gelu_a * h * h * h))
    return 0.5 * h * (1.0 + t)


def gelu_slope(h):
    t = jnp.tanh(gelu_c * (h + gelu_a * h * h * h))
    return 0.5 * (1.0 + t) + 0.5 * h * (1.0 - t * t) * gelu_c * (1.0 + 3.0 * gelu_a * h * h)


def rounded(v):
    return lax.optimization_barrier(v.astype(jnp.bfloat16)).astype(jnp.float32)


def reference(inputs, w_in, w_out, y_cot):
    feat_blk = D // N_ROW
    unit_blk = FF // N_COL
    group = TOK_DEV * N_ROW
    hidden = jnp.zeros((TOKENS, FF), jnp.float32)
    act_grad = jnp.zeros((TOKENS, FF), jnp.float32)
    for r in range(N_ROW):
        lo = r * feat_blk
        hidden = hidden + rounded(jnp.dot(inputs[:, lo:lo + feat_blk], w_in[lo:lo + feat_blk, :], preferred_element_type=jnp.float32))
        act_grad = act_grad + rounded(jnp.dot(y_cot[:, lo:lo + feat_blk], w_out[:, lo:lo + feat_blk].T, preferred_element_type=jnp.float32))
    act = gelu_value(hidden).astype(jnp.bfloat16)
    hidden_grad = (act_grad * gelu_slope(hidden)).astype(jnp.bfloat16)
    y_total = jnp.zeros((TOKENS, D), jnp.float32)
    x_total = jnp.zeros((TOKENS, D), jnp.float32)
    for c in range(N_COL):
        lo = c * unit_blk
        y_total = y_total + rounded(jnp.dot(act[:, lo:lo + unit_blk], w_out[lo:lo + unit_blk, :], preferred_element_type=jnp.float32))
        x_total = x_total + rounded(jnp.dot(hidden_grad[:, lo:lo + unit_blk], w_in[:, lo:lo + unit_blk].T, preferred_element_type=jnp.float32))
    w_in_total = jnp.zeros((D, FF), jnp.float32)
    w_out_total = jnp.zeros((FF, D), jnp.float32)
    for g in range(N_DEPTH):
        lo = g * group
        w_in_total = w_in_total + rounded(jnp.dot(inputs[lo:lo + group].T, hidden_grad[lo:lo + group], preferred_element_type=jnp.float32))
        w_out_total = w_out_total + rounded(jnp.dot(act[lo:lo + group].T, y_cot[lo:lo + group], preferred_element_type=jnp.float32))
    return (y_total.astype(jnp.bfloat16), x_total.astype(jnp.bfloat16), w_in_total.astype(jnp.bfloat16), w_out_total.astype(jnp.bfloat16))
```

```python
import jax
import jax.numpy as jnp
from jax import lax
from jax.sharding import PartitionSpec as P

gelu_c = 0.7978845608
gelu_a = 0.044715


def gelu_pair(h):
    t = jnp.tanh(gelu_c * (h + gelu_a * h * h * h))
    value = 0.5 * h * (1.0 + t)
    slope = 0.5 * (1.0 + t) + 0.5 * h * (1.0 - t * t) * gelu_c * (1.0 + 3.0 * gelu_a * h * h)
    return value, slope


def scatter_sum(terms, axis, count):
    blocks = terms.astype(jnp.bfloat16).reshape((count, -1) + terms.shape[1:])
    got = lax.all_to_all(blocks, axis, 0, 0, tiled=True)
    return jnp.sum(got.astype(jnp.float32), axis=0)


def dot(a, b, spec):
    return jnp.einsum(spec, a, b, preferred_element_type=jnp.float32)


def per_device(inputs, w_in, w_out, y_cot):
    n_row, n_col = 4, 16
    x_t = lax.all_gather(inputs.T, "col", axis=0, tiled=True)
    cot_t = lax.all_gather(y_cot.T, "col", axis=0, tiled=True)
    hidden = scatter_sum(dot(x_t, w_in, "dt,df->tf"), "row", n_row)
    value, slope = gelu_pair(hidden)
    act_rows = lax.all_gather(value.astype(jnp.bfloat16), "row", axis=0, tiled=True)
    y_out = scatter_sum(dot(w_out, act_rows, "fd,tf->dt"), "col", n_col)
    act_grad = scatter_sum(dot(cot_t, w_out, "dt,fd->tf"), "row", n_row)
    grad_rows = lax.all_gather((act_grad * slope).astype(jnp.bfloat16), "row", axis=0, tiled=True)
    x_grad = scatter_sum(dot(w_in, grad_rows, "df,tf->dt"), "col", n_col)
    w_in_sum, w_out_sum = lax.psum(
        (
            dot(x_t, grad_rows, "dt,tf->df").astype(jnp.bfloat16),
            dot(act_rows, cot_t, "tf,dt->fd").astype(jnp.bfloat16),
        ),
        "depth",
    )
    return (y_out.astype(jnp.bfloat16).T, x_grad.astype(jnp.bfloat16).T, w_in_sum, w_out_sum)


def solution(mesh):
    in_specs = (
        P("depth", ("row", "col")),
        P("row", "col"),
        P("col", "row"),
        P("depth", ("row", "col")),
    )
    out_specs = (
        P("depth", ("row", "col")),
        P("depth", ("row", "col")),
        P("row", "col"),
        P("col", "row"),
    )
    return jax.shard_map(
        per_device, mesh=mesh, in_specs=in_specs, out_specs=out_specs, check_vma=False
    )
```

```python
import jax
import jax.numpy as jnp
from jax import lax
from jax.sharding import PartitionSpec as P

gelu_c = 0.7978845608
gelu_a = 0.044715
bf16 = jnp.bfloat16
f32 = jnp.float32
n_row, n_col, n_chip = 4, 16, 4


def gelu_pair(h):
    t = jnp.tanh(gelu_c * (h + gelu_a * h * h * h))
    value = 0.5 * h * (1.0 + t)
    slope = 0.5 * (1.0 + t) + 0.5 * h * (1.0 - t * t) * gelu_c * (1.0 + 3.0 * gelu_a * h * h)
    return value, slope


def dot(a, b, spec):
    return jnp.einsum(spec, a, b, preferred_element_type=f32).astype(bf16)


def gather(block, axis):
    return lax.all_gather(block, axis, axis=0, tiled=True)


def scatter_sum(terms, axis, count):
    blocks = terms.reshape((count, -1) + terms.shape[1:])
    got = lax.all_to_all(blocks, axis, 0, 0, tiled=True)
    return jnp.sum(got.astype(f32), axis=0)


def scatter_sum_steps(terms, axis, count):
    blocks = terms.reshape((count, -1) + terms.shape[1:])
    me = lax.axis_index(axis)
    total = lax.dynamic_index_in_dim(blocks, me, 0, keepdims=False).astype(f32)
    for step in (2, 1, 3):
        block = lax.dynamic_index_in_dim(blocks, lax.rem(me + step, count), 0, keepdims=False)
        pairs = [(i, (i + step) % count) for i in range(count)]
        total = total + lax.ppermute(block, axis, pairs).astype(f32)
    return total


def core_half_sum(terms):
    me = lax.axis_index("core")
    halves = terms.reshape((2, -1) + terms.shape[1:])
    mine = lax.dynamic_index_in_dim(halves, me, 0, keepdims=False)
    other = lax.dynamic_index_in_dim(halves, 1 - me, 0, keepdims=False)
    got = lax.ppermute(other, "core", [(0, 1), (1, 0)])
    return (mine.astype(f32) + got.astype(f32)).astype(bf16)


def per_device(inputs, w_in, w_out, y_cot):
    cot_pad = jnp.pad(y_cot.T, ((0, 24), (0, 0)))
    cot_t = lax.all_gather(cot_pad, "col", axis=0)[:, :40].reshape(640, 512)
    x_t = gather(inputs.T, "col")
    hidden = scatter_sum(dot(x_t, w_in, "dt,df->tf"), "row", n_row)
    value, slope = gelu_pair(hidden)
    act_rows = gather(value.astype(bf16), "row")
    y_out = scatter_sum(dot(w_out, act_rows, "fd,tf->dt"), "col", n_col)
    cot_t, _ = lax.optimization_barrier((cot_t, act_rows))
    act_grad = scatter_sum_steps(dot(cot_t, w_out, "dt,fd->tf"), "row", n_row)
    grad_rows = gather((act_grad * slope).astype(bf16), "row")
    x_grad = scatter_sum(dot(w_in, grad_rows, "df,tf->dt"), "col", n_col)
    w_terms = jnp.concatenate(
        [dot(x_t, grad_rows, "dt,tf->df"), dot(act_rows, cot_t, "tf,dt->fd")], 0
    )
    w_terms = w_terms.reshape(2, 2, 320, 640).swapaxes(0, 1).reshape(1280, 640)
    half = core_half_sum(w_terms)
    quarter = scatter_sum_steps(half, "chip", n_chip).astype(bf16)
    half = gather(quarter, "chip")
    w_in_sum = gather(half[:320], "core")
    w_out_sum = gather(half[320:], "core")
    return (y_out.astype(bf16).T, x_grad.astype(bf16).T, w_in_sum, w_out_sum)


def solution(mesh):
    shape = mesh.devices.shape
    fine = jax.sharding.Mesh(
        mesh.devices.reshape(shape[0], shape[1], shape[2] // 2, 2), ("row", "col", "chip", "core")
    )
    depth = ("chip", "core")
    acts = P(depth, ("row", "col"))
    return jax.shard_map(
        per_device,
        mesh=fine,
        in_specs=(acts, P("row", "col"), P("col", "row"), acts),
        out_specs=(acts, acts, P("row", "col"), P("col", "row")),
        check_vma=False,
    )
```

```python
import jax
import jax.numpy as jnp
from jax import lax
from jax.sharding import PartitionSpec as P

gelu_c = 0.7978845608
gelu_a = 0.044715
bf16 = jnp.bfloat16
f32 = jnp.float32
n_row, n_col, n_chip = 4, 16, 4


def gelu_pair(h):
    t = jnp.tanh(gelu_c * (h + gelu_a * h * h * h))
    value = 0.5 * h * (1.0 + t)
    slope = 0.5 * (1.0 + t) + 0.5 * h * (1.0 - t * t) * gelu_c * (1.0 + 3.0 * gelu_a * h * h)
    return value, slope


def dot(a, b, spec):
    return jnp.einsum(spec, a, b, preferred_element_type=f32).astype(bf16)


def gather(block, axis):
    return lax.all_gather(block, axis, axis=0, tiled=True)


def scatter_sum(terms, axis, count):
    blocks = terms.reshape((count, -1) + terms.shape[1:])
    got = lax.all_to_all(blocks, axis, 0, 0, tiled=True)
    return jnp.sum(got.astype(f32), axis=0)


def scatter_sum_steps(terms, axis, count):
    blocks = terms.reshape((count, -1) + terms.shape[1:])
    me = lax.axis_index(axis)
    total = lax.dynamic_index_in_dim(blocks, me, 0, keepdims=False).astype(f32)
    for step in (2, 1, 3):
        block = lax.dynamic_index_in_dim(blocks, lax.rem(me + step, count), 0, keepdims=False)
        pairs = [(i, (i + step) % count) for i in range(count)]
        total = total + lax.ppermute(block, axis, pairs).astype(f32)
    return total


def core_half_sum(terms):
    me = lax.axis_index("core")
    halves = terms.reshape((2, -1) + terms.shape[1:])
    mine = lax.dynamic_index_in_dim(halves, me, 0, keepdims=False)
    other = lax.dynamic_index_in_dim(halves, 1 - me, 0, keepdims=False)
    got = lax.ppermute(other, "core", [(0, 1), (1, 0)])
    return (mine.astype(f32) + got.astype(f32)).astype(bf16)


def spread(block, axis, count):
    copies = jnp.broadcast_to(block[None], (count,) + block.shape)
    return lax.all_to_all(copies, axis, 0, 0, tiled=True).reshape((-1,) + block.shape[1:])


def spread_steps(block, axis, count):
    me = lax.axis_index(axis)
    rows = jnp.zeros((count,) + block.shape, block.dtype)
    rows = lax.dynamic_update_index_in_dim(rows, block, me, 0)
    for step in (2, 1, 3):
        pairs = [(i, (i + step) % count) for i in range(count)]
        got = lax.ppermute(block, axis, pairs)
        rows = lax.dynamic_update_index_in_dim(rows, got, lax.rem(me - step + count, count), 0)
    return rows.reshape((-1,) + block.shape[1:])


def ordered(value, earlier):
    return lax.optimization_barrier((value, earlier))[0]


def per_device(inputs, w_in, w_out, y_cot):
    both = gather(jnp.concatenate([inputs.T, y_cot.T[:16]], 0), "col").reshape(n_col, 56, 512)
    rest = ordered(y_cot.T[16:], both)
    rest = spread(rest, "col", n_col).reshape(n_col, 24, 512)
    x_t = both[:, :40].reshape(640, 512)
    hidden_terms = dot(x_t, w_in, "dt,df->tf")
    cot_t = jnp.concatenate([both[:, 40:], rest], 1).reshape(640, 512)
    grad_terms = dot(cot_t, w_out, "dt,fd->tf")
    terms = jnp.stack([hidden_terms.reshape(4, 128, 640), grad_terms.reshape(4, 128, 640)], 1)
    got = lax.all_to_all(terms, "row", 0, 0, tiled=True).astype(f32)
    sums = jnp.sum(got, axis=0)
    value, slope = gelu_pair(sums[0])
    pair = jnp.stack([value.astype(bf16), (sums[1] * slope).astype(bf16)])
    rows = spread(pair[None], "row", n_row)
    act_rows = rows[:, 0].reshape(512, 640)
    grad_rows = rows[:, 1].reshape(512, 640)
    out_terms = jnp.stack(
        [
            dot(w_out, act_rows, "fd,tf->dt").reshape(16, 40, 512),
            dot(w_in, grad_rows, "df,tf->dt").reshape(16, 40, 512),
        ],
        1,
    )
    out_got = lax.all_to_all(out_terms, "col", 0, 0, tiled=True).astype(f32)
    outs = jnp.sum(out_got, axis=0).astype(bf16)
    w_terms = jnp.stack([dot(x_t, grad_rows, "dt,tf->df"), dot(act_rows, cot_t, "tf,dt->fd")])
    w_terms = w_terms.reshape(2, 2, 320, 640).swapaxes(0, 1).reshape(1280, 640)
    half = core_half_sum(w_terms)
    quarter = scatter_sum_steps(half, "chip", n_chip).astype(bf16)
    half = gather(quarter, "chip")
    w_in_sum = gather(half[:320], "core")
    w_out_sum = gather(half[320:], "core")
    return (outs[0].T, outs[1].T, w_in_sum, w_out_sum)


def solution(mesh):
    shape = mesh.devices.shape
    fine = jax.sharding.Mesh(
        mesh.devices.reshape(shape[0], shape[1], shape[2] // 2, 2), ("row", "col", "chip", "core")
    )
    depth = ("chip", "core")
    acts = P(depth, ("row", "col"))
    return jax.shard_map(
        per_device,
        mesh=fine,
        in_specs=(acts, P("row", "col"), P("col", "row"), acts),
        out_specs=(acts, acts, P("row", "col"), P("col", "row")),
        check_vma=False,
    )
```

```python
import math

import jax
import jax.numpy as jnp
from jax import lax
from jax.experimental import pallas as pl
from jax.experimental.pallas import tpu as pltpu
from jax.sharding import PartitionSpec as P

gelu_c = 0.7978845608
gelu_a = 0.044715
bf16 = jnp.bfloat16
f32 = jnp.float32
n_row, n_col, n_chip = 4, 16, 4


def gelu_pair(h):
    t = jnp.tanh(gelu_c * (h + gelu_a * h * h * h))
    value = 0.5 * h * (1.0 + t)
    slope = 0.5 * (1.0 + t) + 0.5 * h * (1.0 - t * t) * gelu_c * (1.0 + 3.0 * gelu_a * h * h)
    return value, slope


def dot(a, b, spec):
    return jnp.einsum(spec, a, b, preferred_element_type=f32).astype(bf16)


def gather(block, axis):
    return lax.all_gather(block, axis, axis=0, tiled=True)


def scatter_sum(terms, axis, count):
    blocks = terms.reshape((count, -1) + terms.shape[1:])
    got = lax.all_to_all(blocks, axis, 0, 0, tiled=True)
    return jnp.sum(got.astype(f32), axis=0)


def scatter_sum_steps(terms, axis, count):
    blocks = terms.reshape((count, -1) + terms.shape[1:])
    me = lax.axis_index(axis)
    total = lax.dynamic_index_in_dim(blocks, me, 0, keepdims=False).astype(f32)
    for step in (2, 1, 3):
        block = lax.dynamic_index_in_dim(blocks, lax.rem(me + step, count), 0, keepdims=False)
        pairs = [(i, (i + step) % count) for i in range(count)]
        total = total + lax.ppermute(block, axis, pairs).astype(f32)
    return total


def core_half_sum(terms):
    me = lax.axis_index("core")
    halves = terms.reshape((2, -1) + terms.shape[1:])
    mine = lax.dynamic_index_in_dim(halves, me, 0, keepdims=False)
    other = lax.dynamic_index_in_dim(halves, 1 - me, 0, keepdims=False)
    got = lax.ppermute(other, "core", [(0, 1), (1, 0)])
    return (mine.astype(f32) + got.astype(f32)).astype(bf16)


def spread(block, axis, count):
    copies = jnp.broadcast_to(block[None], (count,) + block.shape)
    return lax.all_to_all(copies, axis, 0, 0, tiled=True).reshape((-1,) + block.shape[1:])


def spread_steps(block, axis, count):
    me = lax.axis_index(axis)
    rows = jnp.zeros((count,) + block.shape, block.dtype)
    rows = lax.dynamic_update_index_in_dim(rows, block, me, 0)
    for step in (2, 1, 3):
        pairs = [(i, (i + step) % count) for i in range(count)]
        got = lax.ppermute(block, axis, pairs)
        rows = lax.dynamic_update_index_in_dim(rows, got, lax.rem(me - step + count, count), 0)
    return rows.reshape((-1,) + block.shape[1:])


def ordered(value, earlier):
    return lax.optimization_barrier((value, earlier))[0]


def permute(block, axis, count, step):
    return lax.ppermute(block, axis, [(i, (i + step) % count) for i in range(count)])


vmem = pl.BlockSpec(memory_space=pltpu.VMEM)
smem = pl.BlockSpec(memory_space=pltpu.SMEM)


def kernel_call(body, outs, flops, *args, scratch=()):
    shapes = tuple(jax.ShapeDtypeStruct(shape, bf16) for shape in outs)
    moved = sum(2 * math.prod(a.shape) for a in args) + sum(2 * math.prod(s) for s in outs)
    return pl.pallas_call(
        body,
        out_shape=shapes,
        in_specs=[smem if a.dtype == jnp.int32 else vmem for a in args],
        out_specs=(vmem,) * len(shapes),
        scratch_shapes=[pltpu.VMEM(shape, bf16) for shape in scratch],
        cost_estimate=pl.CostEstimate(flops=flops, bytes_accessed=moved, transcendentals=0),
        compiler_params=pltpu.CompilerParams(vmem_limit_bytes=32 * 1024 * 1024),
    )(*args)


def contract(a, b, dim_a, dim_b):
    return lax.dot_general(a, b, (((dim_a,), (dim_b,)), ((), ())), preferred_element_type=f32)


def first_kernel(x_ref, cot_ref, first_ref, rest_ref):
    for block in range(4):
        first_ref[block] = x_ref[:, block * 128 : (block + 1) * 128]
    for block in range(2):
        first_ref[4 + block] = cot_ref[:, block * 128 : (block + 1) * 128]
        for copy in range(16):
            rest_ref[copy, block] = cot_ref[:, (2 + block) * 128 : (3 + block) * 128]


def hidden_kernel(both_ref, weight_ref, x_ref, terms_ref):
    weight = weight_ref[...]
    for block in range(4):
        rows = both_ref[:, block].reshape(640, 128)
        x_ref[:, block * 128 : (block + 1) * 128] = rows
        terms_ref[block] = contract(rows, weight, 0, 0).astype(bf16)


def grad_kernel(both_ref, rest_ref, weight_ref, hidden_ref, cot_ref, terms_ref):
    weight = weight_ref[...]
    for block in range(4):
        rows = (both_ref[:, 4 + block] if block < 2 else rest_ref[:, block - 2]).reshape(640, 128)
        cot_ref[:, block * 128 : (block + 1) * 128] = rows
        terms_ref[block, 0] = hidden_ref[block]
        terms_ref[block, 1] = contract(rows, weight, 0, 0).astype(bf16)


def out_kernel(out_w_ref, in_w_ref, rows_ref, terms_ref):
    for stream, weight_ref in ((0, out_w_ref), (1, in_w_ref)):
        rows = rows_ref[:, stream].reshape(512, 640)
        terms = contract(weight_ref[...], rows, 1, 1)
        terms_ref[:, stream] = terms.astype(bf16).reshape(16, 40, 512)


def weight_kernel(core_ref, x_ref, cot_ref, rows_ref, mine_ref, other_ref, whole_ref):
    core = core_ref[0]
    whole_ref[0] = contract(x_ref[...], rows_ref[:, 1].reshape(512, 640), 1, 0).astype(bf16)
    whole_ref[1] = contract(rows_ref[:, 0].reshape(512, 640), cot_ref[...], 0, 1).astype(bf16)
    for grad in range(2):
        mine_ref[grad] = whole_ref[grad, pl.ds(pl.multiple_of(core * 320, 320), 320)]
        other_ref[grad] = whole_ref[grad, pl.ds(pl.multiple_of(320 - core * 320, 320), 320)]


def sum_kernel(got_ref, y_ref, x_ref):
    for stream, out_ref in ((0, y_ref), (1, x_ref)):
        total = got_ref[0, stream].astype(f32)
        for source in range(1, 16):
            total = total + got_ref[source, stream].astype(f32)
        out_ref[...] = total.astype(bf16)


def join_kernel(core_ref, mine_ref, other_ref, in_ref, out_ref):
    core = core_ref[0]
    for grad, whole_ref in ((0, in_ref), (1, out_ref)):
        part = slice(grad * 320, (grad + 1) * 320)
        whole_ref[pl.ds(pl.multiple_of(core * 320, 320), 320)] = mine_ref[part]
        whole_ref[pl.ds(pl.multiple_of(320 - core * 320, 320), 320)] = other_ref[part]


def per_device(inputs, w_in, w_out, y_cot):
    core_id = lax.axis_index("core").astype(jnp.int32)[None]
    first, rest = kernel_call(
        first_kernel, [(6, 40, 128), (16, 2, 40, 128)], 0, inputs.T, y_cot.T
    )
    both = gather(first.reshape(240, 128), "col").reshape(16, 6, 40, 128)
    rest = lax.all_to_all(ordered(rest, both).reshape(16, 80, 128), "col", 0, 0, tiled=True)
    out_w = ordered(w_out.T, both)
    x_t, hidden_terms = kernel_call(
        hidden_kernel, [(640, 512), (4, 128, 640)], 2 * 512 * 640 * 640, both, w_in
    )
    cot_t, terms = kernel_call(
        grad_kernel,
        [(640, 512), (4, 2, 128, 640)],
        2 * 512 * 640 * 640,
        both,
        ordered(rest, hidden_terms).reshape(16, 2, 40, 128),
        out_w,
        hidden_terms,
    )
    got = lax.all_to_all(terms, "row", 0, 0, tiled=True).astype(f32)
    hidden, act_grad = jnp.sum(got[:, 0], axis=0), jnp.sum(got[:, 1], axis=0)
    value, slope = gelu_pair(hidden)
    pair = jnp.stack([value.astype(bf16), (act_grad * slope).astype(bf16)])
    rows = spread(pair[None], "row", n_row)
    (out_terms,) = kernel_call(
        out_kernel, [(16, 2, 40, 512)], 4 * 512 * 640 * 640, out_w, w_in, rows
    )
    out_got = lax.all_to_all(out_terms, "col", 0, 0, tiled=True)
    y_t, x_grad_t = kernel_call(sum_kernel, [(40, 512)] * 2, 2 * 16 * 40 * 512, out_got)
    mine, other = kernel_call(
        weight_kernel,
        [(2, 320, 640), (2, 320, 640)],
        4 * 512 * 640 * 640,
        core_id,
        x_t,
        cot_t,
        rows,
        scratch=[(2, 640, 640)],
    )
    got = lax.ppermute(other, "core", [(0, 1), (1, 0)])
    half = (mine.astype(f32) + got.astype(f32)).astype(bf16).reshape(640, 640)
    quarter = scatter_sum_steps(half, "chip", n_chip).astype(bf16)
    half = gather(quarter, "chip")
    other = lax.ppermute(half, "core", [(0, 1), (1, 0)])
    w_in_sum, w_out_sum = kernel_call(join_kernel, [(640, 640)] * 2, 0, core_id, half, other)
    return (y_t.T, x_grad_t.T, w_in_sum, w_out_sum)


def solution(mesh):
    shape = mesh.devices.shape
    fine = jax.sharding.Mesh(
        mesh.devices.reshape(shape[0], shape[1], shape[2] // 2, 2), ("row", "col", "chip", "core")
    )
    depth = ("chip", "core")
    acts = P(depth, ("row", "col"))
    return jax.shard_map(
        per_device,
        mesh=fine,
        in_specs=(acts, P("row", "col"), P("col", "row"), acts),
        out_specs=(acts, acts, P("row", "col"), P("col", "row")),
        check_vma=False,
    )
```

```python
import math

import jax
import jax.numpy as jnp
from jax import lax
from jax.experimental import pallas as pl
from jax.experimental.pallas import tpu as pltpu
from jax.sharding import PartitionSpec as P

gelu_c = 0.7978845608
gelu_a = 0.044715
bf16 = jnp.bfloat16
f32 = jnp.float32
n_row, n_col, n_chip = 4, 16, 4


def gelu_pair(h):
    t = jnp.tanh(gelu_c * (h + gelu_a * h * h * h))
    value = 0.5 * h * (1.0 + t)
    slope = 0.5 * (1.0 + t) + 0.5 * h * (1.0 - t * t) * gelu_c * (1.0 + 3.0 * gelu_a * h * h)
    return value, slope


def dot(a, b, spec):
    return jnp.einsum(spec, a, b, preferred_element_type=f32).astype(bf16)


def gather(block, axis):
    return lax.all_gather(block, axis, axis=0, tiled=True)


def scatter_sum(terms, axis, count):
    blocks = terms.reshape((count, -1) + terms.shape[1:])
    got = lax.all_to_all(blocks, axis, 0, 0, tiled=True)
    return jnp.sum(got.astype(f32), axis=0)


def scatter_sum_steps(terms, axis, count):
    blocks = terms.reshape((count, -1) + terms.shape[1:])
    me = lax.axis_index(axis)
    total = lax.dynamic_index_in_dim(blocks, me, 0, keepdims=False).astype(f32)
    for step in (2, 1, 3):
        block = lax.dynamic_index_in_dim(blocks, lax.rem(me + step, count), 0, keepdims=False)
        pairs = [(i, (i + step) % count) for i in range(count)]
        total = total + lax.ppermute(block, axis, pairs).astype(f32)
    return total


def core_half_sum(terms):
    me = lax.axis_index("core")
    halves = terms.reshape((2, -1) + terms.shape[1:])
    mine = lax.dynamic_index_in_dim(halves, me, 0, keepdims=False)
    other = lax.dynamic_index_in_dim(halves, 1 - me, 0, keepdims=False)
    got = lax.ppermute(other, "core", [(0, 1), (1, 0)])
    return (mine.astype(f32) + got.astype(f32)).astype(bf16)


def spread(block, axis, count):
    copies = jnp.broadcast_to(block[None], (count,) + block.shape)
    return lax.all_to_all(copies, axis, 0, 0, tiled=True).reshape((-1,) + block.shape[1:])


def spread_steps(block, axis, count):
    me = lax.axis_index(axis)
    rows = jnp.zeros((count,) + block.shape, block.dtype)
    rows = lax.dynamic_update_index_in_dim(rows, block, me, 0)
    for step in (2, 1, 3):
        pairs = [(i, (i + step) % count) for i in range(count)]
        got = lax.ppermute(block, axis, pairs)
        rows = lax.dynamic_update_index_in_dim(rows, got, lax.rem(me - step + count, count), 0)
    return rows.reshape((-1,) + block.shape[1:])


def ordered(value, earlier):
    return lax.optimization_barrier((value, earlier))[0]


def permute(block, axis, count, step):
    return lax.ppermute(block, axis, [(i, (i + step) % count) for i in range(count)])


vmem = pl.BlockSpec(memory_space=pltpu.VMEM)
smem = pl.BlockSpec(memory_space=pltpu.SMEM)


def kernel_call(body, outs, flops, *args, scratch=()):
    shapes = tuple(jax.ShapeDtypeStruct(shape, bf16) for shape in outs)
    moved = sum(2 * math.prod(a.shape) for a in args) + sum(2 * math.prod(s) for s in outs)
    return pl.pallas_call(
        body,
        out_shape=shapes,
        in_specs=[smem if a.dtype == jnp.int32 else vmem for a in args],
        out_specs=(vmem,) * len(shapes),
        scratch_shapes=[pltpu.VMEM(shape, bf16) for shape in scratch],
        cost_estimate=pl.CostEstimate(flops=flops, bytes_accessed=moved, transcendentals=0),
        compiler_params=pltpu.CompilerParams(vmem_limit_bytes=32 * 1024 * 1024),
    )(*args)


def contract(a, b, dim_a, dim_b):
    return lax.dot_general(a, b, (((dim_a,), (dim_b,)), ((), ())), preferred_element_type=f32)


def terms_kernel(
    odd_ref, own_ref, x_other_ref, cot_other_ref, in_w_ref, out_w_ref, x_ref, cot_ref, terms_ref
):
    odd = odd_ref[0]
    for stream, other_ref, weight_ref, whole_ref in (
        (0, x_other_ref, in_w_ref, x_ref), (1, cot_other_ref, out_w_ref, cot_ref)
    ):
        for high in range(8):
            whole_ref[2 * high + odd] = own_ref[high, stream * 40 : (stream + 1) * 40]
            whole_ref[2 * high + 1 - odd] = other_ref[high]
        terms = contract(whole_ref[...].reshape(640, 512), weight_ref[...], 0, 0)
        terms_ref[:, stream] = terms.astype(bf16).reshape(4, 128, 640)


def out_kernel(out_w_ref, in_w_ref, rows_ref, terms_ref):
    for stream, weight_ref in ((0, out_w_ref), (1, in_w_ref)):
        rows = rows_ref[:, stream].reshape(512, 640)
        terms = contract(weight_ref[...], rows, 1, 1)
        terms_ref[:, stream] = terms.astype(bf16).reshape(16, 40, 512)


def weight_kernel(core_ref, x_ref, cot_ref, rows_ref, mine_ref, other_ref, whole_ref):
    core = core_ref[0]
    whole_ref[0] = contract(x_ref[...], rows_ref[:, 1].reshape(512, 640), 1, 0).astype(bf16)
    whole_ref[1] = contract(rows_ref[:, 0].reshape(512, 640), cot_ref[...], 0, 1).astype(bf16)
    for grad in range(2):
        mine_ref[grad] = whole_ref[grad, pl.ds(pl.multiple_of(core * 320, 320), 320)]
        other_ref[grad] = whole_ref[grad, pl.ds(pl.multiple_of(320 - core * 320, 320), 320)]


def sum_kernel(got_ref, y_ref, x_ref):
    for stream, out_ref in ((0, y_ref), (1, x_ref)):
        total = got_ref[0, stream].astype(f32)
        for source in range(1, got_ref.shape[0]):
            total = total + got_ref[source, stream].astype(f32)
        out_ref[...] = total.astype(bf16)


def join_kernel(core_ref, in_mine_ref, out_mine_ref, in_other_ref, out_other_ref, in_ref, out_ref):
    core = core_ref[0]
    mine = pl.ds(pl.multiple_of(core * 320, 320), 320)
    other = pl.ds(pl.multiple_of(320 - core * 320, 320), 320)
    in_ref[mine] = in_mine_ref[...]
    in_ref[other] = in_other_ref[...]
    out_ref[mine] = out_mine_ref[...]
    out_ref[other] = out_other_ref[...]


def add(a, b):
    return (a.astype(f32) + b.astype(f32)).astype(bf16)


EVEN = [(0, 1), (1, 0), (2, 3), (3, 2)]
ODD = [(1, 2), (2, 1), (3, 0), (0, 3)]


def chip_sum(in_half, out_half):
    in_got, out_got = lax.ppermute(in_half, "chip", EVEN), lax.ppermute(out_half, "chip", ODD)
    in_half, out_half = add(in_half, in_got), add(out_half, out_got)
    in_got, out_got = lax.ppermute(in_half, "chip", ODD), lax.ppermute(out_half, "chip", EVEN)
    return add(in_half, in_got), add(out_half, out_got)


COL = ("high", "low")


def per_device(inputs, w_in, w_out, y_cot):
    core_id = lax.axis_index("core").astype(jnp.int32)[None]
    odd = lax.axis_index("low").astype(jnp.int32)[None]
    both = jnp.concatenate([inputs.T, y_cot.T], 0)
    far = lax.all_gather(both, "high", axis=0)
    x_other = permute(far[:, :40], COL, 16, 1)
    cot_other = permute(far[:, 40:], COL, 16, 15)
    out_w = ordered(w_out.T, far)
    x_t, cot_t, terms = kernel_call(
        terms_kernel,
        [(16, 40, 512), (16, 40, 512), (4, 2, 128, 640)],
        4 * 512 * 640 * 640,
        odd,
        far,
        x_other,
        cot_other,
        w_in,
        out_w,
    )
    x_t, cot_t = x_t.reshape(640, 512), cot_t.reshape(640, 512)
    got = lax.all_to_all(terms, "row", 0, 0, tiled=True).astype(f32)
    hidden, act_grad = jnp.sum(got[:, 0], axis=0), jnp.sum(got[:, 1], axis=0)
    value, slope = gelu_pair(hidden)
    pair = jnp.stack([value.astype(bf16), (act_grad * slope).astype(bf16)])
    rows = spread(pair[None], "row", n_row)
    (out_terms,) = kernel_call(
        out_kernel, [(16, 2, 40, 512)], 4 * 512 * 640 * 640, out_w, w_in, rows
    )
    out_got = lax.all_to_all(out_terms, COL, 0, 0, tiled=True)
    y_t, x_grad_t = kernel_call(sum_kernel, [(40, 512)] * 2, 2 * 16 * 40 * 512, out_got)
    mine, other = kernel_call(
        weight_kernel,
        [(2, 320, 640), (2, 320, 640)],
        4 * 512 * 640 * 640,
        core_id,
        x_t,
        cot_t,
        rows,
        scratch=[(2, 640, 640)],
    )
    got = lax.ppermute(other, "core", [(0, 1), (1, 0)])
    in_half, out_half = chip_sum(add(mine[0], got[0]), add(mine[1], got[1]))
    in_other = lax.ppermute(in_half, "core", [(0, 1), (1, 0)])
    out_other = lax.ppermute(out_half, "core", [(0, 1), (1, 0)])
    w_in_sum, w_out_sum = kernel_call(
        join_kernel, [(640, 640)] * 2, 0, core_id, in_half, out_half, in_other, out_other
    )
    return (y_t.T, x_grad_t.T, w_in_sum, w_out_sum)


def solution(mesh):
    shape = mesh.devices.shape
    fine = jax.sharding.Mesh(
        mesh.devices.reshape(shape[0], shape[1] // 2, 2, shape[2] // 2, 2),
        ("row", "high", "low", "chip", "core"),
    )
    depth = ("chip", "core")
    acts = P(depth, ("row",) + COL)
    return jax.shard_map(
        per_device,
        mesh=fine,
        in_specs=(acts, P("row", COL), P(COL, "row"), acts),
        out_specs=(acts, acts, P("row", COL), P(COL, "row")),
        check_vma=False,
    )
```

```python
import math

import jax
import jax.numpy as jnp
from jax import lax
from jax.experimental import pallas as pl
from jax.experimental.pallas import tpu as pltpu
from jax.sharding import PartitionSpec as P

gelu_c = 0.7978845608
gelu_a = 0.044715
bf16 = jnp.bfloat16
f32 = jnp.float32
COL = ("high", "low")
SWAP = [(0, 1), (1, 0)]
EVEN = [(0, 1), (1, 0), (2, 3), (3, 2)]
ODD = [(1, 2), (2, 1), (3, 0), (0, 3)]


def gelu_pair(h):
    t = jnp.tanh(gelu_c * (h + gelu_a * h * h * h))
    value = 0.5 * h * (1.0 + t)
    slope = 0.5 * (1.0 + t) + 0.5 * h * (1.0 - t * t) * gelu_c * (1.0 + 3.0 * gelu_a * h * h)
    return value, slope


def ordered(value, earlier):
    return lax.optimization_barrier((value, earlier))[0]


def permute(block, axis, count, step):
    return lax.ppermute(block, axis, [(i, (i + step) % count) for i in range(count)])


def spread(block, axis, count):
    copies = jnp.broadcast_to(block[None], (count,) + block.shape)
    return lax.all_to_all(copies, axis, 0, 0, tiled=True)


def add(a, b):
    return (a.astype(f32) + b.astype(f32)).astype(bf16)


def chip_sum(in_half, out_half):
    in_got, out_got = lax.ppermute(in_half, "chip", EVEN), lax.ppermute(out_half, "chip", ODD)
    in_half, out_half = add(in_half, in_got), add(out_half, out_got)
    in_got, out_got = lax.ppermute(in_half, "chip", ODD), lax.ppermute(out_half, "chip", EVEN)
    return add(in_half, in_got), add(out_half, out_got)


vmem = pl.BlockSpec(memory_space=pltpu.VMEM)
smem = pl.BlockSpec(memory_space=pltpu.SMEM)


def kernel_call(body, outs, flops, *args, scratch=()):
    shapes = tuple(jax.ShapeDtypeStruct(shape, bf16) for shape in outs)
    moved = sum(2 * math.prod(a.shape) for a in args) + sum(2 * math.prod(s) for s in outs)
    return pl.pallas_call(
        body,
        out_shape=shapes,
        in_specs=[smem if a.dtype == jnp.int32 else vmem for a in args],
        out_specs=(vmem,) * len(shapes),
        scratch_shapes=[pltpu.VMEM(shape, bf16) for shape in scratch],
        cost_estimate=pl.CostEstimate(flops=flops, bytes_accessed=moved, transcendentals=0),
        compiler_params=pltpu.CompilerParams(vmem_limit_bytes=32 * 1024 * 1024),
    )(*args)


def contract(a, b, dim_a, dim_b):
    return lax.dot_general(a, b, (((dim_a,), (dim_b,)), ((), ())), preferred_element_type=f32)


def terms_kernel(
    odd_ref, own_ref, cot_other_ref, x_other_ref, in_w_ref, out_w_ref, x_ref, cot_ref, terms_ref
):
    odd = odd_ref[0]
    for stream, other_ref, weight_ref, whole_ref in (
        (0, x_other_ref, in_w_ref, x_ref), (1, cot_other_ref, out_w_ref, cot_ref)
    ):
        for high in range(8):
            whole_ref[2 * high + odd] = own_ref[high, stream * 40 : (stream + 1) * 40]
            whole_ref[2 * high + 1 - odd] = other_ref[high]
        terms = contract(whole_ref[...].reshape(640, 512), weight_ref[...], 0, 0)
        terms_ref[:, stream] = terms.astype(bf16).reshape(4, 128, 640)


def out_kernel(out_w_ref, in_w_ref, rows_ref, terms_ref):
    for stream, weight_ref in ((0, out_w_ref), (1, in_w_ref)):
        rows = rows_ref[:, stream].reshape(512, 640)
        terms = contract(weight_ref[...], rows, 1, 1)
        terms_ref[:, stream] = terms.astype(bf16).reshape(16, 40, 512)


def weight_kernel(core_ref, x_ref, cot_ref, rows_ref, mine_ref, other_ref, whole_ref):
    core = core_ref[0]
    whole_ref[0] = contract(x_ref[...], rows_ref[:, 1].reshape(512, 640), 1, 0).astype(bf16)
    whole_ref[1] = contract(rows_ref[:, 0].reshape(512, 640), cot_ref[...], 0, 1).astype(bf16)
    for grad in range(2):
        mine_ref[grad] = whole_ref[grad, pl.ds(pl.multiple_of(core * 320, 320), 320)]
        other_ref[grad] = whole_ref[grad, pl.ds(pl.multiple_of(320 - core * 320, 320), 320)]


def sum_kernel(got_ref, y_ref, x_ref):
    for stream, out_ref in ((0, y_ref), (1, x_ref)):
        total = got_ref[0, stream].astype(f32)
        for source in range(1, got_ref.shape[0]):
            total = total + got_ref[source, stream].astype(f32)
        out_ref[...] = total.astype(bf16)


def join_kernel(core_ref, in_mine_ref, out_mine_ref, in_other_ref, out_other_ref, in_ref, out_ref):
    core = core_ref[0]
    mine = pl.ds(pl.multiple_of(core * 320, 320), 320)
    other = pl.ds(pl.multiple_of(320 - core * 320, 320), 320)
    in_ref[mine] = in_mine_ref[...]
    in_ref[other] = in_other_ref[...]
    out_ref[mine] = out_mine_ref[...]
    out_ref[other] = out_other_ref[...]


def per_device(inputs, w_in, w_out, y_cot):
    core_id = lax.axis_index("core").astype(jnp.int32)[None]
    odd = lax.axis_index("low").astype(jnp.int32)[None]
    both = jnp.concatenate([inputs.T, y_cot.T], 0)
    far = lax.all_gather(both, "high", axis=0)
    x_other = permute(far[:, :40], COL, 16, 1)
    cot_other = permute(far[:, 40:], COL, 16, 15)
    out_w = ordered(w_out.T, far)
    x_t, cot_t, terms = kernel_call(
        terms_kernel,
        [(16, 40, 512), (16, 40, 512), (4, 2, 128, 640)],
        4 * 512 * 640 * 640,
        odd,
        far,
        cot_other,
        x_other,
        w_in,
        out_w,
    )
    x_t, cot_t = x_t.reshape(640, 512), cot_t.reshape(640, 512)
    got = lax.all_to_all(terms, "row", 0, 0, tiled=True).astype(f32)
    hidden, act_grad = jnp.sum(got[:, 0], axis=0), jnp.sum(got[:, 1], axis=0)
    value, slope = gelu_pair(hidden)
    pair = jnp.stack([value.astype(bf16), (act_grad * slope).astype(bf16)])
    rows = spread(pair, "row", 4)
    (out_terms,) = kernel_call(
        out_kernel,
        [(16, 2, 40, 512)],
        4 * 512 * 640 * 640,
        out_w,
        w_in,
        rows,
    )
    out_got = lax.all_to_all(out_terms, COL, 0, 0, tiled=True)
    y_t, x_grad_t = kernel_call(sum_kernel, [(40, 512)] * 2, 2 * 16 * 40 * 512, out_got)
    mine, other = kernel_call(
        weight_kernel,
        [(2, 320, 640), (2, 320, 640)],
        4 * 512 * 640 * 640,
        core_id,
        x_t,
        cot_t,
        rows,
        scratch=[(2, 640, 640)],
    )
    got = lax.ppermute(other, "core", SWAP)
    in_half, out_half = chip_sum(add(mine[0], got[0]), add(mine[1], got[1]))
    in_other = lax.ppermute(in_half, "core", SWAP)
    out_other = lax.ppermute(out_half, "core", SWAP)
    w_in_sum, w_out_sum = kernel_call(
        join_kernel, [(640, 640)] * 2, 0, core_id, in_half, out_half, in_other, out_other
    )
    return (y_t.T, x_grad_t.T, w_in_sum, w_out_sum)


def solution(mesh):
    shape = mesh.devices.shape
    fine = jax.sharding.Mesh(
        mesh.devices.reshape(shape[0], shape[1] // 2, 2, shape[2] // 2, 2),
        ("row", "high", "low", "chip", "core"),
    )
    depth = ("chip", "core")
    acts = P(depth, ("row",) + COL)
    return jax.shard_map(
        per_device,
        mesh=fine,
        in_specs=(acts, P("row", COL), P(COL, "row"), acts),
        out_specs=(acts, acts, P("row", COL), P(COL, "row")),
        check_vma=False,
    )
```

```python
import math

import jax
import jax.numpy as jnp
from jax import lax
from jax.experimental import pallas as pl
from jax.experimental.pallas import tpu as pltpu
from jax.sharding import PartitionSpec as P

gelu_c = 0.7978845608
gelu_a = 0.044715
bf16 = jnp.bfloat16
f32 = jnp.float32
COL = ("high", "low")
SWAP = [(0, 1), (1, 0)]
EVEN = [(0, 1), (1, 0), (2, 3), (3, 2)]
ODD = [(1, 2), (2, 1), (3, 0), (0, 3)]


def gelu_pair(h):
    t = jnp.tanh(gelu_c * (h + gelu_a * h * h * h))
    value = 0.5 * h * (1.0 + t)
    slope = 0.5 * (1.0 + t) + 0.5 * h * (1.0 - t * t) * gelu_c * (1.0 + 3.0 * gelu_a * h * h)
    return value, slope


def ordered(value, earlier):
    return lax.optimization_barrier((value, earlier))[0]


def permute(block, axis, count, step):
    return lax.ppermute(block, axis, [(i, (i + step) % count) for i in range(count)])


def add(a, b):
    return (a.astype(f32) + b.astype(f32)).astype(bf16)


def chip_sum(in_half, out_half):
    in_got, out_got = lax.ppermute(in_half, "chip", EVEN), lax.ppermute(out_half, "chip", ODD)
    in_half, out_half = add(in_half, in_got), add(out_half, out_got)
    in_got, out_got = lax.ppermute(in_half, "chip", ODD), lax.ppermute(out_half, "chip", EVEN)
    return add(in_half, in_got), add(out_half, out_got)


vmem = pl.BlockSpec(memory_space=pltpu.VMEM)
smem = pl.BlockSpec(memory_space=pltpu.SMEM)


def kernel_call(body, outs, flops, *args, scratch=(), copies=0, limit=32):
    shapes = tuple(jax.ShapeDtypeStruct(shape, bf16) for shape in outs)
    moved = sum(2 * math.prod(a.shape) for a in args) + sum(2 * math.prod(s) for s in outs)
    return pl.pallas_call(
        body,
        out_shape=shapes,
        in_specs=[smem if a.dtype == jnp.int32 else vmem for a in args],
        out_specs=(pl.BlockSpec(memory_space=pl.ANY) if copies else vmem,) * len(shapes),
        scratch_shapes=[pltpu.VMEM(shape, bf16) for shape in scratch]
        + [pltpu.SemaphoreType.DMA] * copies,
        cost_estimate=pl.CostEstimate(flops=flops, bytes_accessed=moved, transcendentals=0),
        compiler_params=pltpu.CompilerParams(vmem_limit_bytes=limit * 1024 * 1024),
    )(*args)


def contract(a, b, dim_a, dim_b):
    return lax.dot_general(a, b, (((dim_a,), (dim_b,)), ((), ())), preferred_element_type=f32)


def terms_kernel(
    odd_ref, own_ref, cot_other_ref, x_other_ref, in_w_ref, out_w_ref, x_ref, cot_ref, terms_ref
):
    odd = odd_ref[0]
    for stream, other_ref, weight_ref, whole_ref in (
        (0, x_other_ref, in_w_ref, x_ref), (1, cot_other_ref, out_w_ref, cot_ref)
    ):
        for high in range(8):
            whole_ref[2 * high + odd] = own_ref[high, stream * 40 : (stream + 1) * 40]
            whole_ref[2 * high + 1 - odd] = other_ref[high]
        terms = contract(whole_ref[...].reshape(640, 512), weight_ref[...], 0, 0)
        terms_ref[:, stream] = terms.astype(bf16).reshape(4, 128, 640)


def gelu_kernel(got_ref, rows_ref):
    hidden, act_grad = got_ref[0, 0].astype(f32), got_ref[0, 1].astype(f32)
    for source in range(1, 4):
        hidden = hidden + got_ref[source, 0].astype(f32)
        act_grad = act_grad + got_ref[source, 1].astype(f32)
    value, slope = gelu_pair(hidden)
    act, hidden_grad = value.astype(bf16), (act_grad * slope).astype(bf16)
    for target in range(4):
        rows_ref[target, 0] = act
        rows_ref[target, 1] = hidden_grad


def out_kernel(out_w_ref, in_w_ref, rows_ref, terms_ref, *parts):
    copies = []
    for number, (part_ref, sem) in enumerate(zip(parts[:4], parts[4:])):
        stream, half = divmod(number, 2)
        weight = (out_w_ref, in_w_ref)[stream][half * 320 : (half + 1) * 320]
        terms = contract(weight, rows_ref[:, stream].reshape(512, 640), 1, 1)
        part_ref[...] = terms.astype(bf16).reshape(8, 40, 512)
        place = terms_ref.at[half * 8 : (half + 1) * 8, stream]
        copies.append(pltpu.make_async_copy(part_ref, place, sem))
        copies[-1].start()
    for copy in copies:
        copy.wait()


def weight_kernel(core_ref, x_ref, cot_ref, rows_ref, mine_ref, other_ref, whole_ref):
    core = core_ref[0]
    whole_ref[0] = contract(x_ref[...], rows_ref[:, 1].reshape(512, 640), 1, 0).astype(bf16)
    whole_ref[1] = contract(rows_ref[:, 0].reshape(512, 640), cot_ref[...], 0, 1).astype(bf16)
    for grad in range(2):
        mine_ref[grad] = whole_ref[grad, pl.ds(pl.multiple_of(core * 320, 320), 320)]
        other_ref[grad] = whole_ref[grad, pl.ds(pl.multiple_of(320 - core * 320, 320), 320)]


def sum_kernel(got_ref, y_ref, x_ref):
    for stream, out_ref in ((0, y_ref), (1, x_ref)):
        total = got_ref[0, stream].astype(f32)
        for source in range(1, got_ref.shape[0]):
            total = total + got_ref[source, stream].astype(f32)
        out_ref[...] = total.astype(bf16)


def join_kernel(core_ref, in_mine_ref, out_mine_ref, in_other_ref, out_other_ref, in_ref, out_ref):
    core = core_ref[0]
    mine = pl.ds(pl.multiple_of(core * 320, 320), 320)
    other = pl.ds(pl.multiple_of(320 - core * 320, 320), 320)
    in_ref[mine] = in_mine_ref[...]
    in_ref[other] = in_other_ref[...]
    out_ref[mine] = out_mine_ref[...]
    out_ref[other] = out_other_ref[...]


def per_device(inputs, w_in, w_out, y_cot):
    core_id = lax.axis_index("core").astype(jnp.int32)[None]
    odd = lax.axis_index("low").astype(jnp.int32)[None]
    both = jnp.concatenate([inputs.T, y_cot.T], 0)
    far = lax.all_gather(both, "high", axis=0)
    x_other = permute(far[:, :40], COL, 16, 1)
    cot_other = permute(far[:, 40:], COL, 16, 15)
    out_w = ordered(w_out.T, far)
    x_t, cot_t, terms = kernel_call(
        terms_kernel,
        [(16, 40, 512), (16, 40, 512), (4, 2, 128, 640)],
        4 * 512 * 640 * 640,
        odd,
        far,
        cot_other,
        x_other,
        w_in,
        out_w,
    )
    x_t, cot_t = x_t.reshape(640, 512), cot_t.reshape(640, 512)
    got = lax.all_to_all(terms, "row", 0, 0, tiled=True)
    (copies,) = kernel_call(gelu_kernel, [(4, 2, 128, 640)], 30 * 128 * 640, got, limit=8)
    rows = lax.all_to_all(copies, "row", 0, 0, tiled=True)
    (out_terms,) = kernel_call(
        out_kernel,
        [(16, 2, 40, 512)],
        4 * 512 * 640 * 640,
        out_w,
        w_in,
        rows,
        scratch=[(8, 40, 512)] * 4,
        copies=4,
    )
    out_got = lax.all_to_all(out_terms, COL, 0, 0, tiled=True)
    y_t, x_grad_t = kernel_call(sum_kernel, [(40, 512)] * 2, 2 * 16 * 40 * 512, out_got)
    mine, other = kernel_call(
        weight_kernel,
        [(2, 320, 640), (2, 320, 640)],
        4 * 512 * 640 * 640,
        core_id,
        x_t,
        cot_t,
        rows,
        scratch=[(2, 640, 640)],
    )
    got = lax.ppermute(other, "core", SWAP)
    in_half, out_half = chip_sum(add(mine[0], got[0]), add(mine[1], got[1]))
    in_other = lax.ppermute(in_half, "core", SWAP)
    out_other = lax.ppermute(out_half, "core", SWAP)
    w_in_sum, w_out_sum = kernel_call(
        join_kernel, [(640, 640)] * 2, 0, core_id, in_half, out_half, in_other, out_other
    )
    return (y_t.T, x_grad_t.T, w_in_sum, w_out_sum)


def solution(mesh):
    shape = mesh.devices.shape
    fine = jax.sharding.Mesh(
        mesh.devices.reshape(shape[0], shape[1] // 2, 2, shape[2] // 2, 2),
        ("row", "high", "low", "chip", "core"),
    )
    depth = ("chip", "core")
    acts = P(depth, ("row",) + COL)
    return jax.shard_map(
        per_device,
        mesh=fine,
        in_specs=(acts, P("row", COL), P(COL, "row"), acts),
        out_specs=(acts, acts, P("row", COL), P(COL, "row")),
        check_vma=False,
    )
```

```python
import math

import jax
import jax.numpy as jnp
from jax import lax
from jax.experimental import pallas as pl
from jax.experimental.pallas import tpu as pltpu
from jax.sharding import PartitionSpec as P

gelu_c = 0.7978845608
gelu_a = 0.044715
bf16 = jnp.bfloat16
f32 = jnp.float32
COL = ("high", "low")
SWAP = [(0, 1), (1, 0)]
EVEN = [(0, 1), (1, 0), (2, 3), (3, 2)]
ODD = [(1, 2), (2, 1), (3, 0), (0, 3)]


def gelu_pair(h):
    t = jnp.tanh(gelu_c * (h + gelu_a * h * h * h))
    value = 0.5 * h * (1.0 + t)
    slope = 0.5 * (1.0 + t) + 0.5 * h * (1.0 - t * t) * gelu_c * (1.0 + 3.0 * gelu_a * h * h)
    return value, slope


def ordered(value, earlier):
    return lax.optimization_barrier((value, earlier))[0]


def permute(block, axis, count, step):
    return lax.ppermute(block, axis, [(i, (i + step) % count) for i in range(count)])


def add(a, b):
    return (a.astype(f32) + b.astype(f32)).astype(bf16)


def chip_sum(in_half, out_half):
    in_got, out_got = lax.ppermute(in_half, "chip", EVEN), lax.ppermute(out_half, "chip", ODD)
    in_half, out_half = add(in_half, in_got), add(out_half, out_got)
    in_got, out_got = lax.ppermute(in_half, "chip", ODD), lax.ppermute(out_half, "chip", EVEN)
    return add(in_half, in_got), add(out_half, out_got)


vmem = pl.BlockSpec(memory_space=pltpu.VMEM)
smem = pl.BlockSpec(memory_space=pltpu.SMEM)


def kernel_call(body, outs, flops, *args, scratch=(), copies=0, limit=32):
    shapes = tuple(jax.ShapeDtypeStruct(shape, bf16) for shape in outs)
    moved = sum(2 * math.prod(a.shape) for a in args) + sum(2 * math.prod(s) for s in outs)
    return pl.pallas_call(
        body,
        out_shape=shapes,
        in_specs=[smem if a.dtype == jnp.int32 else vmem for a in args],
        out_specs=(pl.BlockSpec(memory_space=pl.ANY) if copies else vmem,) * len(shapes),
        scratch_shapes=[pltpu.VMEM(shape, bf16) for shape in scratch]
        + [pltpu.SemaphoreType.DMA] * copies,
        cost_estimate=pl.CostEstimate(flops=flops, bytes_accessed=moved, transcendentals=0),
        compiler_params=pltpu.CompilerParams(vmem_limit_bytes=limit * 1024 * 1024),
    )(*args)


def contract(a, b, dim_a, dim_b):
    return lax.dot_general(a, b, (((dim_a,), (dim_b,)), ((), ())), preferred_element_type=f32)


def terms_kernel(
    odd_ref, own_ref, cot_other_ref, x_other_ref, in_w_ref, out_w_ref, x_ref, cot_ref, terms_ref
):
    odd = odd_ref[0]
    for stream, other_ref, weight_ref, whole_ref in (
        (0, x_other_ref, in_w_ref, x_ref), (1, cot_other_ref, out_w_ref, cot_ref)
    ):
        for high in range(8):
            whole_ref[2 * high + odd] = own_ref[high, stream * 40 : (stream + 1) * 40]
            whole_ref[2 * high + 1 - odd] = other_ref[high]
        terms = contract(whole_ref[...].reshape(640, 512), weight_ref[...], 0, 0)
        terms_ref[:, stream] = terms.astype(bf16).reshape(4, 128, 640)


def gelu_kernel(got_ref, rows_ref):
    hidden, act_grad = got_ref[0, 0].astype(f32), got_ref[0, 1].astype(f32)
    for source in range(1, 4):
        hidden = hidden + got_ref[source, 0].astype(f32)
        act_grad = act_grad + got_ref[source, 1].astype(f32)
    value, slope = gelu_pair(hidden)
    act, hidden_grad = value.astype(bf16), (act_grad * slope).astype(bf16)
    for target in range(4):
        rows_ref[target, 0] = act
        rows_ref[target, 1] = hidden_grad


def out_kernel(out_w_ref, in_w_ref, rows_ref, terms_ref, *parts):
    copies = []
    for number, (part_ref, sem) in enumerate(zip(parts[:8], parts[8:])):
        stream, part = divmod(number, 4)
        weight = (out_w_ref, in_w_ref)[stream][part * 160 : (part + 1) * 160]
        terms = contract(weight, rows_ref[:, stream].reshape(512, 640), 1, 1)
        part_ref[...] = terms.astype(bf16).reshape(4, 40, 512)
        place = terms_ref.at[part * 4 : (part + 1) * 4, stream]
        copies.append(pltpu.make_async_copy(part_ref, place, sem))
        copies[-1].start()
    for copy in copies:
        copy.wait()


def weight_kernel(core_ref, x_ref, cot_ref, rows_ref, mine_ref, other_ref, whole_ref):
    core = core_ref[0]
    whole_ref[0] = contract(x_ref[...], rows_ref[:, 1].reshape(512, 640), 1, 0).astype(bf16)
    whole_ref[1] = contract(rows_ref[:, 0].reshape(512, 640), cot_ref[...], 0, 1).astype(bf16)
    for grad in range(2):
        mine_ref[grad] = whole_ref[grad, pl.ds(pl.multiple_of(core * 320, 320), 320)]
        other_ref[grad] = whole_ref[grad, pl.ds(pl.multiple_of(320 - core * 320, 320), 320)]


def sum_kernel(got_ref, y_ref, x_ref):
    for stream, out_ref in ((0, y_ref), (1, x_ref)):
        total = got_ref[0, stream].astype(f32)
        for source in range(1, got_ref.shape[0]):
            total = total + got_ref[source, stream].astype(f32)
        out_ref[...] = total.astype(bf16)


def join_kernel(core_ref, in_mine_ref, out_mine_ref, in_other_ref, out_other_ref, in_ref, out_ref):
    core = core_ref[0]
    mine = pl.ds(pl.multiple_of(core * 320, 320), 320)
    other = pl.ds(pl.multiple_of(320 - core * 320, 320), 320)
    in_ref[mine] = in_mine_ref[...]
    in_ref[other] = in_other_ref[...]
    out_ref[mine] = out_mine_ref[...]
    out_ref[other] = out_other_ref[...]


def per_device(inputs, w_in, w_out, y_cot):
    core_id = lax.axis_index("core").astype(jnp.int32)[None]
    odd = lax.axis_index("low").astype(jnp.int32)[None]
    both = jnp.concatenate([inputs.T, y_cot.T], 0)
    far = lax.all_gather(both, "high", axis=0)
    x_other = permute(far[:, :40], COL, 16, 1)
    cot_other = permute(far[:, 40:], COL, 16, 15)
    out_w = ordered(w_out.T, far)
    x_t, cot_t, terms = kernel_call(
        terms_kernel,
        [(16, 40, 512), (16, 40, 512), (4, 2, 128, 640)],
        4 * 512 * 640 * 640,
        odd,
        far,
        cot_other,
        x_other,
        w_in,
        out_w,
    )
    x_t, cot_t = x_t.reshape(640, 512), cot_t.reshape(640, 512)
    got = lax.all_to_all(terms, "row", 0, 0, tiled=True)
    (copies,) = kernel_call(gelu_kernel, [(4, 2, 128, 640)], 30 * 128 * 640, got, limit=8)
    rows = lax.all_to_all(copies, "row", 0, 0, tiled=True)
    (out_terms,) = kernel_call(
        out_kernel,
        [(16, 2, 40, 512)],
        4 * 512 * 640 * 640,
        out_w,
        w_in,
        rows,
        scratch=[(4, 40, 512)] * 8,
        copies=8,
    )
    out_got = lax.all_to_all(out_terms, COL, 0, 0, tiled=True)
    y_t, x_grad_t = kernel_call(sum_kernel, [(40, 512)] * 2, 2 * 16 * 40 * 512, out_got)
    mine, other = kernel_call(
        weight_kernel,
        [(2, 320, 640), (2, 320, 640)],
        4 * 512 * 640 * 640,
        core_id,
        x_t,
        cot_t,
        rows,
        scratch=[(2, 640, 640)],
    )
    got = lax.ppermute(other, "core", SWAP)
    in_half, out_half = chip_sum(add(mine[0], got[0]), add(mine[1], got[1]))
    in_other = lax.ppermute(in_half, "core", SWAP)
    out_other = lax.ppermute(out_half, "core", SWAP)
    w_in_sum, w_out_sum = kernel_call(
        join_kernel, [(640, 640)] * 2, 0, core_id, in_half, out_half, in_other, out_other
    )
    return (y_t.T, x_grad_t.T, w_in_sum, w_out_sum)


def solution(mesh):
    shape = mesh.devices.shape
    fine = jax.sharding.Mesh(
        mesh.devices.reshape(shape[0], shape[1] // 2, 2, shape[2] // 2, 2),
        ("row", "high", "low", "chip", "core"),
    )
    depth = ("chip", "core")
    acts = P(depth, ("row",) + COL)
    return jax.shard_map(
        per_device,
        mesh=fine,
        in_specs=(acts, P("row", COL), P(COL, "row"), acts),
        out_specs=(acts, acts, P("row", COL), P(COL, "row")),
        check_vma=False,
    )
```
